32 devices in a mesh: grp: 2 (over y), freq: 4 (over z), ell: 2 (over x), pol: 2 (over core).
Axes of the slice: x: 2, y: 2, z: 4, core: 2. Of those that a mesh axis runs over, the one named last changes fastest.
Arguments:
- beam_matrix: bfloat16 [8, 2, 512, 8192], P(('grp', 'freq'), None, None, ('ell', 'pol')), parts along dimension 0, may hold values from -0.375 to 0.375
- sky_spectrum: float32 [8, 3, 8192], P(('grp', 'freq'), None, ('ell', 'pol')), parts along dimension 0, may hold values from 0.1 to 10
- taper_tiles: bfloat16 [3, 512, 512], P(None, ('ell', 'pol')), may hold values from 0.5 to 1.5
- noise_tiles: bfloat16 [8, 3, 512, 2, 512], P(('grp', 'freq'), None, ('ell', 'pol')), parts along dimension 0, may hold values from -4 to 4
Outputs:
- covariance: float32 [8, 3, 512, 2, 512], P(('grp', 'freq'), None, ('ell', 'pol')), parts along dimension 0
The draws below stay inside these ranges and needn't reach their ends.
There are 2 independent parts, one for each index of `grp`. The reference program is written for one: setup_inputs(seed, part) draws one part's arguments, and reference() takes and returns one part's arrays. A program takes and returns all parts, laid end to end along the dimension named above; an argument that names none is the same for every part. Nothing has to cross between parts.
All inputs are finite; a program needn't handle non-finite values.
Results may differ from the reference program's by a relative error of at most 0.012.
Values may be sent and summed in bfloat16 or wider, within the bound.
No kernel may reach another device: no remote copies, remote signals or barrier semaphores. Data moves between devices by JAX's collectives and lax.ppermute only.
A program may use at most 64 MiB of HBM per device.

```python
import math
import jax
import jax.numpy as jnp
from jax import lax

MODES = 512
LPOL = 8192
SEPS = 3
NFREQ = 4
N_ELL = 2
N_POL = 2


def raised(array, key, source, target, blocks, factor):
    def block_of(position):
        return (jnp.arange(array.shape[position]) // (array.shape[position] // blocks)).reshape((-1,) + (1,) * (array.ndim - 1 - position))

    near = jax.random.permutation(key, blocks)[block_of(target)]
    other_side = (block_of(target) + blocks // 2) % blocks
    return jnp.where((block_of(source) == near) | (block_of(source) == other_side), factor * array, array)


def block_levels(stream_key, dims, pieces, low, top_value):
    factor_of, own = 1.0, jax.random.fold_in(stream_key, 6)
    for position, parts in pieces:
        draws = jnp.exp(jax.random.uniform(jax.random.fold_in(own, position), (parts,), jnp.float32, low / len(pieces), top_value / len(pieces)))
        factor_of = factor_of * jnp.repeat(draws, dims[position] // parts).reshape([-1 if axis == position else 1 for axis in range(len(dims))])
    return factor_of


def centred(rng, dims, deviation, most, cuts=(), held_as=jnp.bfloat16):
    loudness = block_levels(rng, dims, cuts, -0.22, 0.18) if cuts else 1.0
    values = jax.random.normal(rng, dims, jnp.float32) * deviation * loudness
    return jnp.minimum(jnp.maximum(values, -most), most).astype(held_as)


def bell_draw_with(rng, extent, deviation, reach, cuts, heavy, held_as=jnp.bfloat16):
    drawn = deviation * jax.random.normal(rng, extent, jnp.float32)
    if cuts:
        drawn = drawn * block_levels(rng, extent, cuts, -0.22, 0.18)
    return jnp.clip(raised(drawn, jax.random.fold_in(rng, 3), *heavy), -reach, reach).astype(held_as)


def setup_inputs(seed: int = 0, part: int = 0) -> dict:
    keys = jax.random.split(jax.random.key(seed), 5)
    part_splits = jax.random.split(jax.random.fold_in(keys[4], part), 5)
    beam_matrix = bell_draw_with(part_splits[0], (NFREQ, 2, MODES, LPOL), (LPOL // 16) ** -0.5, 0.375, ((0, 4), (3, 4)), (3, 2, 4, 2.0))
    sky_spectrum = jnp.clip(jnp.exp(math.log(10.0) - 4.6051702 * jax.random.uniform(part_splits[1], (NFREQ, SEPS, LPOL), jnp.float32) ** block_levels(part_splits[1], (NFREQ, SEPS, LPOL), ((0, 4), (2, 4)), -0.2, 0.2)), 0.1, 10.0)
    taper_tiles = jnp.clip(0.5 + 1.0 * jax.random.uniform(keys[2], (SEPS, MODES, MODES), jnp.float32) ** block_levels(keys[2], (SEPS, MODES, MODES), ((1, 4),), -0.2, 0.2), 0.5, 1.5).astype(jnp.bfloat16)
    noise_tiles = centred(part_splits[3], (NFREQ, SEPS, MODES, 2, MODES), 0.5, 4.0, ((0, 4), (2, 4)))
    return dict(beam_matrix=beam_matrix, sky_spectrum=sky_spectrum, taper_tiles=taper_tiles, noise_tiles=noise_tiles)


def tile_sum(own_beam, spec_row, partner):
    mode_count = own_beam.shape[1]
    multipoles = own_beam.shape[2]
    group_count = N_ELL * N_POL
    group_width = multipoles // group_count
    scaled = (spec_row[None, None, :] * own_beam.astype(jnp.float32)).astype(jnp.bfloat16)
    scaled = lax.optimization_barrier(scaled)
    left_wide = scaled.astype(jnp.float32).reshape(2, mode_count, group_count, group_width)
    right_wide = partner.astype(jnp.float32).reshape(2, mode_count, group_count, group_width)
    real_part = jnp.einsum("mgl,ngl->gmn", left_wide[0], right_wide[0]) + jnp.einsum("mgl,ngl->gmn", left_wide[1], right_wide[1])
    imag_part = jnp.einsum("mgl,ngl->gmn", left_wide[1], right_wide[0]) - jnp.einsum("mgl,ngl->gmn", left_wide[0], right_wide[1])
    partials = jnp.stack([real_part, imag_part], axis=2).astype(jnp.bfloat16)
    partials = lax.optimization_barrier(partials)
    return jnp.sum(partials.astype(jnp.float32), axis=0)


def reference(beam_matrix, sky_spectrum, taper_tiles, noise_tiles):
    freq_total = beam_matrix.shape[0]

    def one_freq(bundle):
        own_beam, spec_rows, noise_rows, freq_index = bundle
        per_sep = []
        for sep_index in range(SEPS):
            target = freq_index + sep_index + 1
            picked = jnp.minimum(target, freq_total - 1).astype(jnp.int32)
            partner = lax.dynamic_index_in_dim(beam_matrix, picked, 0, keepdims=False)
            partner = jnp.where(target < freq_total, partner, jnp.zeros_like(partner))
            summed = tile_sum(own_beam, spec_rows[sep_index], partner)
            per_sep.append(taper_tiles[sep_index].astype(jnp.float32)[:, None, :] * summed + noise_rows[sep_index].astype(jnp.float32))
        return jnp.stack(per_sep)

    indices = jnp.arange(freq_total, dtype=jnp.int32)
    return lax.map(one_freq, (beam_matrix, sky_spectrum, noise_tiles, indices))
```

```python
import jax
import jax.numpy as jnp
from jax import lax
from jax.experimental import pallas as pl
from jax.experimental.pallas import tpu as pltpu
from jax.sharding import PartitionSpec as P

LANES = 128
DOWN, UP = 0, 1
LOW, HIGH = 1, 2


def passed_along(block, axis, distance):
    devices = range(lax.axis_size(axis))
    route = [(i - distance, i) for i in devices if i - distance in devices]
    return lax.ppermute(block, axis, route)


def tile_term(scaled, stacked_right):
    real_rows, imag_rows = scaled[0], scaled[1]
    top_half = jnp.concatenate([real_rows, imag_rows], axis=-1)
    bottom_half = jnp.concatenate([imag_rows, -real_rows], axis=-1)
    rows = real_rows.shape[0]
    left_rows = jnp.stack([top_half, bottom_half], axis=1).reshape(2 * rows, -1)
    product = lax.dot_general(
        left_rows, stacked_right, (((1,), (1,)), ((), ())), preferred_element_type=jnp.float32
    )
    return product.reshape(rows, 2, -1)


def partners_passed_down(beam_matrix, sky_spectrum, taper_tiles, noise_tiles):
    separations = sky_spectrum.shape[1]
    terms = []
    for sep in range(separations):
        partner = passed_along(beam_matrix, "freq", -(sep + 1))[0]
        scaled = sky_spectrum[0, sep][None, None, :] * beam_matrix[0].astype(jnp.float32)
        right = jnp.concatenate([partner[0], partner[1]], axis=-1)
        term = tile_term(scaled.astype(jnp.bfloat16), right).astype(jnp.bfloat16)
        term = lax.psum_scatter(term, ("ell", "pol"), scatter_dimension=0, tiled=True)
        terms.append(term.astype(jnp.float32))
    summed = jnp.stack(terms)[None]
    taper = taper_tiles.astype(jnp.float32)[None, :, :, None, :]
    return taper * summed + noise_tiles.astype(jnp.float32)


def products_body(steps, columns, cores, place_ref, spec_ref, *refs):
    x_refs, (y_ref, keep_ref, send_ref, both_ref) = refs[:-4], refs[-4:]
    side, column = place_ref[0], place_ref[1]
    mode_count = x_refs[0].shape[1]
    chunk_rows = y_ref.shape[2]
    per_device = mode_count // (columns * cores)
    piece = chunk_rows // (columns * cores)
    band = cores * per_device
    contract_last = (((1,), (1,)), ((), ()))
    for slot, (x, chunk, spec) in enumerate(steps):
        x_ref = x_refs[x]
        y = y_ref[chunk].reshape(2 * chunk_rows, y_ref.shape[3])
        y = (y.astype(jnp.float32) * spec_ref[pl.ds(spec, 1), :]).astype(jnp.bfloat16)
        for e in range(columns):
            rows = pl.ds(e * band, band)
            z0 = lax.dot_general(
                x_ref[0, rows, :], y, contract_last, preferred_element_type=jnp.float32
            )
            z1 = lax.dot_general(
                x_ref[1, rows, :], y, contract_last, preferred_element_type=jnp.float32
            )
            real = z0[:, :chunk_rows] + z1[:, chunk_rows:]
            imag = z1[:, :chunk_rows] - z0[:, chunk_rows:]

            @pl.when(side == DOWN)
            def _():
                for c in range(cores):
                    own = slice(c * per_device, (c + 1) * per_device)
                    both_ref[e, slot, c, 0] = real[own].astype(jnp.bfloat16)
                    both_ref[e, slot, c, 1] = imag[own].astype(jnp.bfloat16)

            @pl.when(side == UP)
            def _():
                for part, value in ((0, real), (1, -imag)):
                    for b in range(band // LANES):
                        block = value[b * LANES : (b + 1) * LANES].T.astype(jnp.bfloat16)
                        at = (e * (band // LANES) + b) * piece
                        for d in range(columns * cores):
                            both_ref[d // cores, slot, d % cores, part, at : at + piece] = block[
                                d * piece : (d + 1) * piece
                            ]

    keep_ref[...] = both_ref[column]
    send_ref[...] = both_ref[1 - column]


def products(steps, place, specs, xs, y, columns, cores):
    mode_count = xs[0].shape[1]
    chunk_rows = y.shape[2]
    held = (len(steps), cores, 2, mode_count // (columns * cores), chunk_rows)
    width = y.shape[3]
    flops = len(steps) * 8 * mode_count * chunk_rows * width
    vmem = pl.BlockSpec(memory_space=pltpu.VMEM)

    def body(*refs):
        products_body(steps, columns, cores, *refs)

    return pl.pallas_call(
        body,
        out_shape=[jax.ShapeDtypeStruct(held, jnp.bfloat16)] * 2,
        in_specs=[pl.BlockSpec(memory_space=pltpu.SMEM)] + [vmem] * (len(xs) + 2),
        out_specs=[vmem, vmem],
        scratch_shapes=[pltpu.VMEM((columns,) + held, jnp.bfloat16)],
        compiler_params=pltpu.CompilerParams(vmem_limit_bytes=32 * 2**20),
        cost_estimate=pl.CostEstimate(
            flops=flops, bytes_accessed=2 * width * 2 * (len(xs) * mode_count), transcendentals=0
        ),
    )(place, specs, *xs, y)


def meet_in_the_middle(beam_matrix, sky_spectrum, taper_tiles, noise_tiles):
    columns, cores = lax.axis_size("ell"), lax.axis_size("pol")
    freqs = lax.axis_size("freq")
    freq, column, side = (lax.axis_index(name) for name in ("freq", "ell", "pol"))
    own = beam_matrix[0]
    mode_count, width = own.shape[1], own.shape[2]
    sharers = columns * cores
    per_device = mode_count // sharers
    chunks = mode_count // LANES
    piece = LANES // sharers
    down = side == DOWN
    place = jnp.stack([side, column]).astype(jnp.int32)

    def along(block, route):
        pairs = [(f * cores + p, g * cores + q) for (f, p), (g, q) in route]
        return lax.ppermute(block, ("freq", "pol"), pairs)

    def over_columns(block, members):
        pairs = [
            ((f * columns + e) * cores + p, (f * columns + 1 - e) * cores + p)
            for f, p in members
            for e in range(columns)
        ]
        return lax.ppermute(block, ("freq", "ell", "pol"), pairs)

    def other_core(block):
        return lax.ppermute(block, "pol", [(0, 1), (1, 0)])

    def chunk_of(k):
        straight = own[:, k * LANES : (k + 1) * LANES]
        spread = own.reshape(2, sharers, per_device, width)[:, :, k * piece : (k + 1) * piece]
        return jnp.where(down, straight, spread.reshape(2, LANES, width))

    middle = [(LOW, DOWN), (HIGH, UP)]
    first, last = 0, freqs - 1

    below = lax.ppermute(sky_spectrum[0], "freq", [(f, f + 1) for f in range(freqs - 1)])
    below2 = lax.ppermute(sky_spectrum[0], "freq", [(f, f + 2) for f in range(freqs - 2)])

    outer = along(
        own,
        [
            ((first, DOWN), (LOW, DOWN)),
            ((last, UP), (HIGH, UP)),
            ((LOW, UP), (first, UP)),
            ((HIGH, DOWN), (last, DOWN)),
        ],
    )
    own_chunks = [chunk_of(k) for k in range(chunks)]
    near = [
        along(c, [((HIGH, DOWN), (LOW, DOWN)), ((LOW, UP), (HIGH, UP))]) for c in own_chunks
    ]
    far_chunks, outer = lax.optimization_barrier((own_chunks, outer))
    far = [
        along(c, [((last, DOWN), (LOW, DOWN)), ((first, UP), (HIGH, UP))]) for c in far_chunks
    ]

    own_sky = sky_spectrum[0]
    near_spec = jnp.where(
        down, jnp.stack([below[1], own_sky[0]]), jnp.stack([below[1], below[0]])
    )
    far_spec = jnp.where(
        down, jnp.stack([below[2], own_sky[1]]), jnp.stack([below2[2], below2[1]])
    )
    end_spec = jnp.where(down, below[:1], own_sky[:1])

    def summed(kept, sent, members):
        arrived = over_columns(sent, members)
        return (kept.astype(jnp.float32) + arrived.astype(jnp.float32)).astype(jnp.bfloat16)

    def pair(y, specs):
        steps = [(0, 0, 0), (1, 0, 1)]
        return products(steps, place, specs, [outer, own], y[None], columns, cores)

    end_steps = [(0, k, 0) for k in range(chunks)]
    end_sum = summed(
        *products(end_steps, place, end_spec, [outer], jnp.stack(own_chunks), columns, cores),
        middle + [(first, UP), (last, DOWN)],
    )
    end_back = along(end_sum, [((LOW, DOWN), (first, DOWN)), ((last, DOWN), (HIGH, DOWN))])
    end_home = jnp.where(down, end_back, end_sum)

    at_low = (freq == LOW) & down
    near_home, far_home = [], []
    for block in near:
        total = summed(*pair(block, near_spec), middle)
        back = along(total, [((LOW, DOWN), (first, DOWN)), ((HIGH, UP), (LOW, UP))])
        near_home.append(jnp.where(at_low, total, back))
    for block in far:
        total = summed(*pair(block, far_spec), middle)
        back = along(total, [((LOW, DOWN), (first, DOWN)), ((HIGH, UP), (first, UP))])
        far_home.append(jnp.where(at_low, total, back))

    def exchanged(home):
        kept = lax.dynamic_index_in_dim(home, side, 1, keepdims=False)
        arrived = other_core(lax.dynamic_index_in_dim(home, 1 - side, 1, keepdims=False))
        return jnp.where(down, kept, arrived), jnp.where(down, arrived, kept)

    def straight_tile(parts):
        return jnp.stack(parts).transpose(2, 1, 0, 3).reshape(per_device, 2, mode_count)

    def spread_tile(parts):
        stacked = jnp.stack(parts).reshape(chunks, 2, mode_count // LANES, piece, LANES)
        return stacked.transpose(0, 3, 1, 2, 4).reshape(per_device, 2, mode_count)

    end_d, end_u = exchanged(end_home)
    near_d, near_u = zip(*[exchanged(h) for h in near_home])
    far_d, far_u = zip(*[exchanged(h) for h in far_home])
    zero = jnp.zeros((per_device, 2, mode_count), jnp.float32)

    def total_of(d_parts, u_parts):
        return straight_tile(d_parts).astype(jnp.float32) + spread_tile(u_parts).astype(
            jnp.float32
        )

    end_tile = total_of([end_d[k] for k in range(chunks)], [end_u[k] for k in range(chunks)])
    at_first, at_lower = freq == first, freq == LOW
    sum0 = jnp.where(
        at_lower,
        total_of([c[1] for c in near_d], [c[1] for c in near_u]),
        jnp.where(freq == last, zero, end_tile),
    )
    sum1 = jnp.where(
        at_first,
        total_of([c[0] for c in near_d], [c[1] for c in far_u]),
        jnp.where(at_lower, total_of([c[1] for c in far_d], [c[0] for c in near_u]), zero),
    )
    sum2 = jnp.where(at_first, total_of([c[0] for c in far_d], [c[0] for c in far_u]), zero)
    tiles = jnp.stack([sum0, sum1, sum2])
    taper = taper_tiles.astype(jnp.float32)[:, :, None, :]
    return (taper * tiles + noise_tiles[0].astype(jnp.float32))[None]


def local(beam_matrix, sky_spectrum, taper_tiles, noise_tiles):
    freqs, columns, cores = (lax.axis_size(name) for name in ("freq", "ell", "pol"))
    separations = sky_spectrum.shape[1]
    mode_count = beam_matrix.shape[2]
    two_below_two_above = freqs == 2 * HIGH and separations == freqs - 1
    halves = columns == 2 and cores == 2
    whole_pieces = mode_count % (LANES * columns * cores) == 0
    if two_below_two_above and halves and whole_pieces:
        return meet_in_the_middle(beam_matrix, sky_spectrum, taper_tiles, noise_tiles)
    return partners_passed_down(beam_matrix, sky_spectrum, taper_tiles, noise_tiles)


def solution(mesh):
    placed = (
        P(("grp", "freq"), None, None, ("ell", "pol")),
        P(("grp", "freq"), None, ("ell", "pol")),
        P(None, ("ell", "pol"), None),
        P(("grp", "freq"), None, ("ell", "pol"), None, None),
    )
    return jax.shard_map(
        local,
        mesh=mesh,
        in_specs=placed,
        out_specs=P(("grp", "freq"), None, ("ell", "pol"), None, None),
        check_vma=False,
    )
```

```python
import jax
import jax.numpy as jnp
from jax import lax
from jax.experimental import pallas as pl
from jax.experimental.pallas import tpu as pltpu
from jax.sharding import PartitionSpec as P

LANES = 128
DOWN, UP = 0, 1
LOW, HIGH = 1, 2


def passed_along(block, axis, distance):
    devices = range(lax.axis_size(axis))
    route = [(i - distance, i) for i in devices if i - distance in devices]
    return lax.ppermute(block, axis, route)


def tile_term(scaled, stacked_right):
    real_rows, imag_rows = scaled[0], scaled[1]
    top_half = jnp.concatenate([real_rows, imag_rows], axis=-1)
    bottom_half = jnp.concatenate([imag_rows, -real_rows], axis=-1)
    rows = real_rows.shape[0]
    left_rows = jnp.stack([top_half, bottom_half], axis=1).reshape(2 * rows, -1)
    product = lax.dot_general(
        left_rows, stacked_right, (((1,), (1,)), ((), ())), preferred_element_type=jnp.float32
    )
    return product.reshape(rows, 2, -1)


def partners_passed_down(beam_matrix, sky_spectrum, taper_tiles, noise_tiles):
    separations = sky_spectrum.shape[1]
    terms = []
    for sep in range(separations):
        partner = passed_along(beam_matrix, "freq", -(sep + 1))[0]
        scaled = sky_spectrum[0, sep][None, None, :] * beam_matrix[0].astype(jnp.float32)
        right = jnp.concatenate([partner[0], partner[1]], axis=-1)
        term = tile_term(scaled.astype(jnp.bfloat16), right).astype(jnp.bfloat16)
        term = lax.psum_scatter(term, ("ell", "pol"), scatter_dimension=0, tiled=True)
        terms.append(term.astype(jnp.float32))
    summed = jnp.stack(terms)[None]
    taper = taper_tiles.astype(jnp.float32)[None, :, :, None, :]
    return taper * summed + noise_tiles.astype(jnp.float32)


CONTRACT_LAST = (((1,), (1,)), ((), ()))


def complex_product(left, right):
    rows, columns, width = left.shape[1], right.shape[1], left.shape[2]
    z = lax.dot_general(
        left.reshape(2 * rows, width),
        right.reshape(2 * columns, width),
        CONTRACT_LAST,
        preferred_element_type=jnp.float32,
    )
    real = z[:rows, :columns] + z[rows:, columns:]
    imag = z[rows:, :columns] - z[:rows, columns:]
    return real.astype(jnp.bfloat16), imag.astype(jnp.bfloat16)


def weighted(block, spectrum):
    return (block.astype(jnp.float32) * spectrum).astype(jnp.bfloat16)


def on_each_side(side, run):
    pl.when(side == DOWN)(lambda: run(False))
    pl.when(side == UP)(lambda: run(True))


def whole_tiles_body(steps, columns, cores, place_ref, spec_ref, *refs):
    blocks, (keep_ref, send_ref, both_ref) = refs[:-3], refs[-3:]
    mode_count = blocks[0].shape[1]
    per_device = mode_count // (columns * cores)

    def run(up):
        for tile, (x, y, spec) in enumerate(steps):
            for k in range(columns * cores):
                band = slice(k * per_device, (k + 1) * per_device)
                part_y = weighted(blocks[y][:, band], spec_ref[spec : spec + 1])
                if up:
                    product = complex_product(part_y, blocks[x][...])
                    for part in range(2):
                        both_ref[k // cores, tile, k % cores, part] = product[part]
                else:
                    product = complex_product(blocks[x][...], part_y)
                    for part in range(2):
                        for d in range(columns * cores):
                            rows = slice(d * per_device, (d + 1) * per_device)
                            both_ref[d // cores, tile, d % cores, part, :, band] = product[part][rows]

    on_each_side(place_ref[0], run)
    keep_ref[...] = both_ref[place_ref[1]]
    send_ref[...] = both_ref[1 - place_ref[1]]


def chunk_tiles_body(columns, cores, place_ref, spec_ref, *refs):
    blocks, (y_ref, keep_ref, send_ref, both_ref) = refs[:-4], refs[-4:]
    mode_count = blocks[0].shape[1]
    sharers = columns * cores
    per_device = mode_count // sharers
    piece = LANES // sharers

    def run(up):
        for slot in range(len(blocks)):
            for sub in range(y_ref.shape[0]):
                part_y = weighted(y_ref[sub], spec_ref[slot : slot + 1])
                if up:
                    product = complex_product(part_y, blocks[slot][...])
                else:
                    product = complex_product(blocks[slot][...], part_y)
                for part in range(2):
                    for d in range(sharers):
                        at = (d // cores, d % cores, slot, sub, part)
                        if not up:
                            rows = slice(d * per_device, (d + 1) * per_device)
                            both_ref[at] = product[part][rows]
                            continue
                        share = product[part][d * piece : (d + 1) * piece]
                        for b in range(mode_count // LANES):
                            rows = slice(b * piece, (b + 1) * piece)
                            both_ref[at + (rows,)] = share[:, b * LANES : (b + 1) * LANES]

    on_each_side(place_ref[0], run)
    keep_ref[...] = both_ref[place_ref[1]]
    send_ref[...] = both_ref[1 - place_ref[1]]


def kernel_call(body, held, columns, place, specs, arrays):
    vmem = pl.BlockSpec(memory_space=pltpu.VMEM)
    return pl.pallas_call(
        body,
        out_shape=[jax.ShapeDtypeStruct(held, jnp.bfloat16)] * 2,
        in_specs=[pl.BlockSpec(memory_space=pltpu.SMEM)] + [vmem] * (len(arrays) + 1),
        out_specs=[vmem, vmem],
        scratch_shapes=[pltpu.VMEM((columns,) + held, jnp.bfloat16)],
        compiler_params=pltpu.CompilerParams(vmem_limit_bytes=24 * 2**20),
        cost_estimate=pl.CostEstimate(flops=0, bytes_accessed=0, transcendentals=0),
    )(place, specs, *arrays)


def assemble_body(freqs, cores, place_ref, taper_ref, noise_ref, *refs):
    *refs, out_ref = refs
    whole_kept, whole_come, *chunk_refs = refs
    chunk_pairs = list(zip(chunk_refs[::2], chunk_refs[1::2]))
    subs = [(kept, come, i) for kept, come in chunk_pairs for i in range(kept.shape[1])]
    side, freq = place_ref[0], place_ref[2]
    down = side == DOWN
    per_device, mode_count = whole_kept.shape[2:]
    piece = per_device // len(subs)

    def of(kept, come, from_down, at):
        first, second = kept[at].astype(jnp.float32), come[at].astype(jnp.float32)
        return jnp.where(down, first, second) if from_down else jnp.where(down, second, first)

    def put(sep, part, rows, cols, value):
        taper = taper_ref[sep, rows, cols].astype(jnp.float32)
        noise = noise_ref[sep, rows, part, cols].astype(jnp.float32)
        out_ref[sep, rows, part, cols] = noise if value is None else taper * value + noise

    def column_chunk(slot, j, k, part):
        kept, come, sub = subs[k]
        rows = slice(j * piece, (j + 1) * piece)
        return of(kept, come, True, (slot, sub, part, rows))

    def row_chunk(slot, j, k, part):
        kept, come, sub = subs[j]
        rows = slice(k * piece, (k + 1) * piece)
        return of(kept, come, False, (slot, sub, part, rows))

    def fill(sep, value_of):
        for part in range(2):
            for j in range(len(subs)):
                for k in range(mode_count // LANES):
                    rows = slice(j * piece, (j + 1) * piece)
                    cols = slice(k * LANES, (k + 1) * LANES)
                    put(sep, part, rows, cols, value_of(part, j, k, rows, cols))

    def both_whole(part, j, k, rows, cols):
        at = (0, part, rows, cols)
        return whole_kept[at].astype(jnp.float32) + whole_come[at].astype(jnp.float32)

    def nothing(part, j, k, rows, cols):
        return None

    def low_second(part, j, k, rows, cols):
        return of(whole_kept, whole_come, True, (1, part, rows, cols)) + row_chunk(1, j, k, part)

    def middle_second(part, j, k, rows, cols):
        return of(whole_kept, whole_come, False, (1, part, rows, cols)) + column_chunk(
            1, j, k, part
        )

    def low_third(part, j, k, rows, cols):
        return column_chunk(0, j, k, part) + row_chunk(0, j, k, part)

    pl.when(freq < freqs - 1)(lambda: fill(0, both_whole))
    pl.when(freq == freqs - 1)(lambda: fill(0, nothing))
    pl.when(freq == 0)(lambda: fill(1, low_second))
    pl.when(freq == LOW)(lambda: fill(1, middle_second))
    pl.when(freq > LOW)(lambda: fill(1, nothing))
    pl.when(freq == 0)(lambda: fill(2, low_third))
    pl.when(freq > 0)(lambda: fill(2, nothing))


def meet_in_the_middle(beam_matrix, sky_spectrum, taper_tiles, noise_tiles):
    columns, cores = lax.axis_size("ell"), lax.axis_size("pol")
    freqs = lax.axis_size("freq")
    freq, column, side = (lax.axis_index(name) for name in ("freq", "ell", "pol"))
    own = beam_matrix[0]
    mode_count, width = own.shape[1], own.shape[2]
    sharers = columns * cores
    per_device = mode_count // sharers
    chunks = mode_count // LANES
    piece = LANES // sharers
    down = side == DOWN
    place = jnp.stack([side, column, freq]).astype(jnp.int32)

    def along(block, route):
        pairs = [(f * cores + p, g * cores + q) for (f, p), (g, q) in route]
        return lax.ppermute(block, ("freq", "pol"), pairs)

    def over_columns(block, members):
        pairs = [
            ((f * columns + e) * cores + p, (f * columns + 1 - e) * cores + p)
            for f, p in members
            for e in range(columns)
        ]
        return lax.ppermute(block, ("freq", "ell", "pol"), pairs)

    def other_core(block):
        return lax.ppermute(block, "pol", [(0, 1), (1, 0)])

    def chunk_of(k):
        straight = own[:, k * LANES : (k + 1) * LANES]
        spread = own.reshape(2, sharers, per_device, width)[:, :, k * piece : (k + 1) * piece]
        return jnp.where(down, straight, spread.reshape(2, LANES, width))

    middle = [(LOW, DOWN), (HIGH, UP)]
    first, last = 0, freqs - 1

    below = lax.ppermute(sky_spectrum[0], "freq", [(f, f + 1) for f in range(freqs - 1)])
    below2 = lax.ppermute(sky_spectrum[0], "freq", [(f, f + 2) for f in range(freqs - 2)])

    outer = along(
        own,
        [
            ((first, DOWN), (LOW, DOWN)),
            ((last, UP), (HIGH, UP)),
            ((LOW, UP), (first, UP)),
            ((HIGH, DOWN), (last, DOWN)),
        ],
    )
    near = along(own, [((HIGH, DOWN), (LOW, DOWN)), ((LOW, UP), (HIGH, UP))])
    cuts = [range(0, chunks // 2)] + [range(k, k + 1) for k in range(chunks // 2, chunks)]
    far_chunks = [jnp.stack([chunk_of(k) for k in cut]) for cut in cuts]
    far_chunks, outer, near, below, below2 = lax.optimization_barrier(
        (far_chunks, outer, near, below, below2)
    )
    far = [
        along(c, [((last, DOWN), (LOW, DOWN)), ((first, UP), (HIGH, UP))]) for c in far_chunks
    ]

    own_sky = sky_spectrum[0]
    whole_specs = jnp.where(
        down,
        jnp.stack([below[0], below[1], own_sky[0]]),
        jnp.stack([own_sky[0], below[1], below[0]]),
    )
    far_specs = jnp.where(
        down, jnp.stack([below[2], own_sky[1]]), jnp.stack([below2[2], below2[1]])
    )

    steps = [(0, 1, 0), (0, 2, 1), (1, 2, 2)]
    held = (len(steps), cores, 2, per_device, mode_count)
    kept, sent = kernel_call(
        lambda *refs: whole_tiles_body(steps, columns, cores, *refs),
        held,
        columns,
        place,
        whole_specs,
        [outer, own, near],
    )
    def far_tiles(y, *earlier):
        y, *_ = lax.optimization_barrier((y, *earlier))
        return kernel_call(
            lambda *refs: chunk_tiles_body(columns, cores, *refs),
            (cores, 2, y.shape[0], 2, per_device, LANES),
            columns,
            place,
            far_specs,
            [outer, own, y],
        )

    def column_sum(pair, members, *later_than):
        arrived = over_columns(pair[1], members)
        kept, arrived, *_ = lax.optimization_barrier((pair[0], arrived, *later_than))
        return (kept.astype(jnp.float32) + arrived.astype(jnp.float32)).astype(jnp.bfloat16)

    at_low = freq == LOW

    def exchanged(by_core):
        kept = lax.dynamic_index_in_dim(by_core, side, 0, keepdims=False)
        return kept, other_core(lax.dynamic_index_in_dim(by_core, 1 - side, 0, keepdims=False))

    pairs = [far_tiles(far[0], kept)]
    pairs.append(far_tiles(far[1], pairs[0][0]))
    whole = column_sum((kept, sent), middle + [(first, UP), (last, DOWN)], pairs[1][0])
    end, near_outer, near_own = whole
    back = along(
        jnp.stack([jnp.where(down, end, near_own), near_outer]),
        [
            ((LOW, DOWN), (first, DOWN)),
            ((HIGH, UP), (LOW, UP)),
            ((last, DOWN), (HIGH, DOWN)),
        ],
    )
    pairs.append(far_tiles(far[2], pairs[1][0], whole))
    totals, backs = [], []
    for pair in pairs:
        totals.append(column_sum(pair, middle, pairs[2][0], *totals[-1:]))
        backs.append(
            along(totals[-1], [((LOW, DOWN), (first, DOWN)), ((HIGH, UP), (first, UP))])
        )
    back, totals[2] = lax.optimization_barrier((back, totals[2]))
    first_sep = jnp.where(
        down, jnp.where(at_low, near_own, back[0]), jnp.where(at_low, back[0], end)
    )
    results = [*exchanged(jnp.stack([first_sep, back[1]], axis=1))]
    for total, back in zip(totals, backs):
        back, *_ = lax.optimization_barrier((back, results[-2]))
        results += exchanged(jnp.where(at_low & down, total, back))

    vmem = pl.BlockSpec(memory_space=pltpu.VMEM)
    covariance = pl.pallas_call(
        lambda *refs: assemble_body(freqs, cores, *refs),
        out_shape=jax.ShapeDtypeStruct(noise_tiles.shape[1:], jnp.float32),
        in_specs=[pl.BlockSpec(memory_space=pltpu.SMEM)] + [vmem] * (len(results) + 2),
        out_specs=vmem,
        compiler_params=pltpu.CompilerParams(vmem_limit_bytes=24 * 2**20),
    )(place, taper_tiles, noise_tiles[0], *results)
    return covariance[None]


def local(beam_matrix, sky_spectrum, taper_tiles, noise_tiles):
    freqs, columns, cores = (lax.axis_size(name) for name in ("freq", "ell", "pol"))
    separations = sky_spectrum.shape[1]
    mode_count = beam_matrix.shape[2]
    two_below_two_above = freqs == 2 * HIGH and separations == freqs - 1
    halves = columns == 2 and cores == 2
    whole_pieces = mode_count % (LANES * columns * cores) == 0
    if two_below_two_above and halves and whole_pieces:
        return meet_in_the_middle(beam_matrix, sky_spectrum, taper_tiles, noise_tiles)
    return partners_passed_down(beam_matrix, sky_spectrum, taper_tiles, noise_tiles)


def solution(mesh):
    placed = (
        P(("grp", "freq"), None, None, ("ell", "pol")),
        P(("grp", "freq"), None, ("ell", "pol")),
        P(None, ("ell", "pol"), None),
        P(("grp", "freq"), None, ("ell", "pol"), None, None),
    )
    return jax.shard_map(
        local,
        mesh=mesh,
        in_specs=placed,
        out_specs=P(("grp", "freq"), None, ("ell", "pol"), None, None),
        check_vma=False,
    )
```

```python
import jax
import jax.numpy as jnp
from jax import lax
from jax.experimental import pallas as pl
from jax.experimental.pallas import tpu as pltpu
from jax.sharding import PartitionSpec as P

LANES = 128
DOWN, UP = 0, 1
LOW, HIGH = 1, 2


def passed_along(block, axis, distance):
    devices = range(lax.axis_size(axis))
    route = [(i - distance, i) for i in devices if i - distance in devices]
    return lax.ppermute(block, axis, route)


def tile_term(scaled, stacked_right):
    real_rows, imag_rows = scaled[0], scaled[1]
    top_half = jnp.concatenate([real_rows, imag_rows], axis=-1)
    bottom_half = jnp.concatenate([imag_rows, -real_rows], axis=-1)
    rows = real_rows.shape[0]
    left_rows = jnp.stack([top_half, bottom_half], axis=1).reshape(2 * rows, -1)
    product = lax.dot_general(
        left_rows, stacked_right, (((1,), (1,)), ((), ())), preferred_element_type=jnp.float32
    )
    return product.reshape(rows, 2, -1)


def partners_passed_down(beam_matrix, sky_spectrum, taper_tiles, noise_tiles):
    separations = sky_spectrum.shape[1]
    terms = []
    for sep in range(separations):
        partner = passed_along(beam_matrix, "freq", -(sep + 1))[0]
        scaled = sky_spectrum[0, sep][None, None, :] * beam_matrix[0].astype(jnp.float32)
        right = jnp.concatenate([partner[0], partner[1]], axis=-1)
        term = tile_term(scaled.astype(jnp.bfloat16), right).astype(jnp.bfloat16)
        term = lax.psum_scatter(term, ("ell", "pol"), scatter_dimension=0, tiled=True)
        terms.append(term.astype(jnp.float32))
    summed = jnp.stack(terms)[None]
    taper = taper_tiles.astype(jnp.float32)[None, :, :, None, :]
    return taper * summed + noise_tiles.astype(jnp.float32)


BAND = 2 * LANES
COST = {1: 2 * 10**9, 2: 4 * 10**9}

CONTRACT_LAST = (((1,), (1,)), ((), ()))


def complex_product(left, right):
    rows, columns, width = left.shape[1], right.shape[1], left.shape[2]
    z = lax.dot_general(
        left.reshape(2 * rows, width),
        right.reshape(2 * columns, width),
        CONTRACT_LAST,
        preferred_element_type=jnp.float32,
    )
    real = z[:rows, :columns] + z[rows:, columns:]
    imag = z[rows:, :columns] - z[:rows, columns:]
    return real.astype(jnp.bfloat16), imag.astype(jnp.bfloat16)


def weighted(block, spectrum):
    return (block.astype(jnp.float32) * spectrum).astype(jnp.bfloat16)


def divided(place_ref, both_ref, keep_ref, send_ref, run):
    side, column, busy = place_ref[0], place_ref[1], place_ref[2] > 0

    def nothing():
        both_ref[...] = jnp.zeros_like(both_ref)

    pl.when(busy & (side == DOWN))(lambda: run(False))
    pl.when(busy & (side == UP))(lambda: run(True))
    pl.when(jnp.logical_not(busy))(nothing)
    keep_ref[...] = both_ref[column]
    send_ref[...] = both_ref[1 - column]


def whole_tiles_body(steps, columns, cores, place_ref, spec_ref, *refs):
    blocks, (keep_ref, send_ref, both_ref) = refs[:-3], refs[-3:]
    mode_count = blocks[0].shape[1]
    per_device = mode_count // (columns * cores)


    def run(up):
        for tile, (x, y) in enumerate(steps):
            left, right = (blocks[y], blocks[x]) if up else (blocks[x], blocks[y])

            @pl.loop(0, mode_count // BAND)
            def _(k):
                band = pl.ds(pl.multiple_of(k * BAND, BAND), BAND)
                part = weighted(right[:, band], spec_ref[tile : tile + 1])
                for kind, product in enumerate(complex_product(left[...], part)):
                    for d in range(columns * cores):
                        share = product[d * per_device : (d + 1) * per_device]
                        both_ref[d // cores, tile, d % cores, kind, :, band] = share

    divided(place_ref, both_ref, keep_ref, send_ref, run)


def chunk_tiles_body(columns, cores, place_ref, spec_ref, *refs):
    blocks, (y_ref, keep_ref, send_ref, both_ref) = refs[:-4], refs[-4:]
    mode_count = blocks[0].shape[1]
    sharers = columns * cores
    per_device = mode_count // sharers
    piece = LANES // sharers

    def run(up):
        for slot in range(len(blocks)):
            for sub in range(y_ref.shape[0]):
                part_y = weighted(y_ref[sub], spec_ref[slot : slot + 1])
                if up:
                    product = complex_product(part_y, blocks[slot][...])
                else:
                    product = complex_product(blocks[slot][...], part_y)
                for part in range(2):
                    for d in range(sharers):
                        at = (d // cores, d % cores, slot, sub, part)
                        if not up:
                            rows = slice(d * per_device, (d + 1) * per_device)
                            both_ref[at] = product[part][rows]
                            continue
                        share = product[part][d * piece : (d + 1) * piece]
                        for b in range(mode_count // LANES):
                            rows = slice(b * piece, (b + 1) * piece)
                            both_ref[at + (rows,)] = share[:, b * LANES : (b + 1) * LANES]

    divided(place_ref, both_ref, keep_ref, send_ref, run)


def kernel_call(body, held, columns, place, specs, arrays, flops):
    vmem = pl.BlockSpec(memory_space=pltpu.VMEM)
    return pl.pallas_call(
        body,
        out_shape=[jax.ShapeDtypeStruct(held, jnp.bfloat16)] * 2,
        in_specs=[pl.BlockSpec(memory_space=pltpu.SMEM)] + [vmem] * (len(arrays) + 1),
        out_specs=[vmem, vmem],
        scratch_shapes=[pltpu.VMEM((columns,) + held, jnp.bfloat16)],
        compiler_params=pltpu.CompilerParams(vmem_limit_bytes=24 * 2**20),
        cost_estimate=pl.CostEstimate(flops=flops, bytes_accessed=0, transcendentals=0),
    )(place, specs, *arrays)


def assemble_body(freqs, cores, place_ref, taper_ref, noise_ref, *refs):
    *refs, out_ref = refs
    whole_kept, whole_come, *chunk_refs = refs
    chunk_pairs = list(zip(chunk_refs[::2], chunk_refs[1::2]))
    subs = [(kept, come, i) for kept, come in chunk_pairs for i in range(kept.shape[1])]
    side, freq = place_ref[0], place_ref[3]
    down = side == DOWN
    per_device, mode_count = whole_kept.shape[2:]
    piece = per_device // len(subs)

    def of(kept, come, from_down, at):
        first, second = kept[at].astype(jnp.float32), come[at].astype(jnp.float32)
        return jnp.where(down, first, second) if from_down else jnp.where(down, second, first)

    def put(sep, part, rows, cols, value):
        taper = taper_ref[sep, rows, cols].astype(jnp.float32)
        noise = noise_ref[sep, rows, part, cols].astype(jnp.float32)
        out_ref[sep, rows, part, cols] = noise if value is None else taper * value + noise

    def column_chunk(slot, j, k, part):
        kept, come, sub = subs[k]
        rows = slice(j * piece, (j + 1) * piece)
        return of(kept, come, True, (slot, sub, part, rows))

    def row_chunk(slot, j, k, part):
        kept, come, sub = subs[j]
        rows = slice(k * piece, (k + 1) * piece)
        return of(kept, come, False, (slot, sub, part, rows))

    def fill(sep, value_of):
        for part in range(2):
            for j in range(len(subs)):
                for k in range(mode_count // LANES):
                    rows = slice(j * piece, (j + 1) * piece)
                    cols = slice(k * LANES, (k + 1) * LANES)
                    put(sep, part, rows, cols, value_of(part, j, k, rows, cols))

    def both_whole(part, j, k, rows, cols):
        at = (0, part, rows, cols)
        return whole_kept[at].astype(jnp.float32) + whole_come[at].astype(jnp.float32)

    def nothing(part, j, k, rows, cols):
        return None

    def low_second(part, j, k, rows, cols):
        return of(whole_kept, whole_come, True, (1, part, rows, cols)) + row_chunk(1, j, k, part)

    def middle_second(part, j, k, rows, cols):
        return of(whole_kept, whole_come, False, (1, part, rows, cols)) + column_chunk(
            1, j, k, part
        )

    def low_third(part, j, k, rows, cols):
        return column_chunk(0, j, k, part) + row_chunk(0, j, k, part)

    pl.when(freq < freqs - 1)(lambda: fill(0, both_whole))
    pl.when(freq == freqs - 1)(lambda: fill(0, nothing))
    pl.when(freq == 0)(lambda: fill(1, low_second))
    pl.when(freq == LOW)(lambda: fill(1, middle_second))
    pl.when(freq > LOW)(lambda: fill(1, nothing))
    pl.when(freq == 0)(lambda: fill(2, low_third))
    pl.when(freq > 0)(lambda: fill(2, nothing))


def meet_in_the_middle(beam_matrix, sky_spectrum, taper_tiles, noise_tiles):
    columns, cores = lax.axis_size("ell"), lax.axis_size("pol")
    freqs = lax.axis_size("freq")
    freq, column, side = (lax.axis_index(name) for name in ("freq", "ell", "pol"))
    own = beam_matrix[0]
    mode_count, width = own.shape[1], own.shape[2]
    sharers = columns * cores
    per_device = mode_count // sharers
    chunks = mode_count // LANES
    piece = LANES // sharers
    down = side == DOWN
    first, last = 0, freqs - 1
    meets = ((freq == LOW) & down) | ((freq == HIGH) & ~down)
    outside = ((freq == first) & ~down) | ((freq == last) & down)

    def place_of(busy):
        return jnp.stack([side, column, busy, freq]).astype(jnp.int32)

    def along(block, route):
        pairs = [(f * cores + p, g * cores + q) for (f, p), (g, q) in route]
        return lax.ppermute(block, ("freq", "pol"), pairs)

    def over_columns(block, members):
        pairs = [
            ((f * columns + e) * cores + p, (f * columns + 1 - e) * cores + p)
            for f, p in members
            for e in range(columns)
        ]
        return lax.ppermute(block, ("freq", "ell", "pol"), pairs)

    def other_core(block):
        return lax.ppermute(block, "pol", [(0, 1), (1, 0)])

    def chunk_of(k):
        straight = own[:, k * LANES : (k + 1) * LANES]
        spread = own.reshape(2, sharers, per_device, width)[:, :, k * piece : (k + 1) * piece]
        return jnp.where(down, straight, spread.reshape(2, LANES, width))

    middle = [(LOW, DOWN), (HIGH, UP)]

    below = lax.ppermute(sky_spectrum[0], "freq", [(f, f + 1) for f in range(freqs - 1)])
    below2 = lax.ppermute(sky_spectrum[0], "freq", [(f, f + 2) for f in range(freqs - 2)])

    outer = along(
        own,
        [
            ((first, DOWN), (LOW, DOWN)),
            ((last, UP), (HIGH, UP)),
            ((LOW, UP), (first, UP)),
            ((HIGH, DOWN), (last, DOWN)),
        ],
    )
    near = along(own, [((HIGH, DOWN), (LOW, DOWN)), ((LOW, UP), (HIGH, UP))])
    cuts = [range(0, chunks // 2)] + [range(k, k + 1) for k in range(chunks // 2, chunks)]
    far_chunks = [jnp.stack([chunk_of(k) for k in cut]) for cut in cuts]
    far_chunks, outer, below, below2 = lax.optimization_barrier(
        (far_chunks, outer, below, below2)
    )
    far = [
        along(c, [((last, DOWN), (LOW, DOWN)), ((first, UP), (HIGH, UP))]) for c in far_chunks
    ]

    own_sky = sky_spectrum[0]
    end_specs = jnp.where(down, below[:1], own_sky[:1])
    near_specs = jnp.where(
        down, jnp.stack([below[1], own_sky[0]]), jnp.stack([below[1], below[0]])
    )
    far_specs = jnp.where(
        down, jnp.stack([below[2], own_sky[1]]), jnp.stack([below2[2], below2[1]])
    )

    def after(value, *earlier):
        return lax.optimization_barrier((value, *earlier))[0]

    def whole_tiles(steps, specs, busy, blocks):
        return kernel_call(
            lambda *refs: whole_tiles_body(steps, columns, cores, *refs),
            (len(steps), cores, 2, per_device, mode_count),
            columns,
            place_of(busy),
            specs,
            blocks,
            flops=COST[len(steps)],
        )

    def far_tiles(y):
        return kernel_call(
            lambda *refs: chunk_tiles_body(columns, cores, *refs),
            (cores, 2, y.shape[0], 2, per_device, LANES),
            columns,
            place_of(meets),
            far_specs,
            [outer, own, y],
            flops=COST[2],
        )

    def swapped(pair, members):
        return pair[0], over_columns(pair[1], members)

    def total(pair):
        return (pair[0].astype(jnp.float32) + pair[1].astype(jnp.float32)).astype(jnp.bfloat16)

    def exchanged(by_core):
        kept = lax.dynamic_index_in_dim(by_core, side, 0, keepdims=False)
        return kept, other_core(lax.dynamic_index_in_dim(by_core, 1 - side, 0, keepdims=False))

    def far_home(sums):
        come = along(sums, [((LOW, DOWN), (first, DOWN)), ((HIGH, UP), (first, UP))])
        return jnp.where(at_low & down, sums, come)

    at_low = freq == LOW
    pair = whole_tiles([(0, 1)], end_specs, meets | outside, [outer, own])
    end = swapped(pair, middle + [(first, UP), (last, DOWN)])
    near = after(near, pair[0])
    pair = whole_tiles([(0, 2), (1, 2)], near_specs, meets, [outer, own, near])
    nears = swapped(pair, middle)
    end = total(after(end, pair[0]))[0]

    far0 = far_tiles(after(far[0], end))
    swap0 = swapped(far0, middle)
    near_outer, near_own = total(after(nears, far0[0]))
    come = along(
        jnp.where(down, end, near_own),
        [((LOW, DOWN), (first, DOWN)), ((HIGH, UP), (LOW, UP)), ((last, DOWN), (HIGH, DOWN))],
    )
    second = along(near_outer, [((LOW, DOWN), (first, DOWN)), ((HIGH, UP), (LOW, UP))])
    far1 = far_tiles(after(far[1], near_outer))
    swap1 = swapped(far1, middle)
    sum0 = total(after(swap0, far1[0]))
    home0 = far_home(sum0)
    far2 = far_tiles(after(far[2], sum0))
    swap2 = swapped(far2, middle)
    sum1 = total(after(swap1, far2[0]))
    home1 = far_home(sum1)
    home2 = far_home(total(after(swap2, sum1)))

    first_sep = jnp.where(
        down, jnp.where(at_low, near_own, come), jnp.where(at_low, come, end)
    )
    results = [*exchanged(jnp.stack([first_sep, second], axis=1))]
    for home in (home0, home1, home2):
        results += exchanged(after(home, results[-2]))

    vmem = pl.BlockSpec(memory_space=pltpu.VMEM)
    covariance = pl.pallas_call(
        lambda *refs: assemble_body(freqs, cores, *refs),
        out_shape=jax.ShapeDtypeStruct(noise_tiles.shape[1:], jnp.float32),
        in_specs=[pl.BlockSpec(memory_space=pltpu.SMEM)] + [vmem] * (len(results) + 2),
        out_specs=vmem,
        compiler_params=pltpu.CompilerParams(vmem_limit_bytes=24 * 2**20),
    )(place_of(meets), taper_tiles, noise_tiles[0], *results)
    return covariance[None]


def local(beam_matrix, sky_spectrum, taper_tiles, noise_tiles):
    freqs, columns, cores = (lax.axis_size(name) for name in ("freq", "ell", "pol"))
    separations = sky_spectrum.shape[1]
    mode_count = beam_matrix.shape[2]
    two_below_two_above = freqs == 2 * HIGH and separations == freqs - 1
    halves = columns == 2 and cores == 2
    whole_pieces = mode_count % (LANES * columns * cores) == 0 and mode_count % BAND == 0
    if two_below_two_above and halves and whole_pieces:
        return meet_in_the_middle(beam_matrix, sky_spectrum, taper_tiles, noise_tiles)
    return partners_passed_down(beam_matrix, sky_spectrum, taper_tiles, noise_tiles)


def solution(mesh):
    placed = (
        P(("grp", "freq"), None, None, ("ell", "pol")),
        P(("grp", "freq"), None, ("ell", "pol")),
        P(None, ("ell", "pol"), None),
        P(("grp", "freq"), None, ("ell", "pol"), None, None),
    )
    return jax.shard_map(
        local,
        mesh=mesh,
        in_specs=placed,
        out_specs=P(("grp", "freq"), None, ("ell", "pol"), None, None),
        check_vma=False,
    )
```

```python
import jax
import jax.numpy as jnp
from jax import lax
from jax.experimental import pallas as pl
from jax.experimental.pallas import tpu as pltpu
from jax.sharding import PartitionSpec as P

LANES = 128
DOWN, UP = 0, 1
LOW, HIGH = 1, 2


def passed_along(block, axis, distance):
    devices = range(lax.axis_size(axis))
    route = [(i - distance, i) for i in devices if i - distance in devices]
    return lax.ppermute(block, axis, route)


def tile_term(scaled, stacked_right):
    real_rows, imag_rows = scaled[0], scaled[1]
    top_half = jnp.concatenate([real_rows, imag_rows], axis=-1)
    bottom_half = jnp.concatenate([imag_rows, -real_rows], axis=-1)
    rows = real_rows.shape[0]
    left_rows = jnp.stack([top_half, bottom_half], axis=1).reshape(2 * rows, -1)
    product = lax.dot_general(
        left_rows, stacked_right, (((1,), (1,)), ((), ())), preferred_element_type=jnp.float32
    )
    return product.reshape(rows, 2, -1)


def partners_passed_down(beam_matrix, sky_spectrum, taper_tiles, noise_tiles):
    separations = sky_spectrum.shape[1]
    terms = []
    for sep in range(separations):
        partner = passed_along(beam_matrix, "freq", -(sep + 1))[0]
        scaled = sky_spectrum[0, sep][None, None, :] * beam_matrix[0].astype(jnp.float32)
        right = jnp.concatenate([partner[0], partner[1]], axis=-1)
        term = tile_term(scaled.astype(jnp.bfloat16), right).astype(jnp.bfloat16)
        term = lax.psum_scatter(term, ("ell", "pol"), scatter_dimension=0, tiled=True)
        terms.append(term.astype(jnp.float32))
    summed = jnp.stack(terms)[None]
    taper = taper_tiles.astype(jnp.float32)[None, :, :, None, :]
    return taper * summed + noise_tiles.astype(jnp.float32)


BAND = 2 * LANES
COST = {1: 2 * 10**9, 2: 4 * 10**9}

CONTRACT_LAST = (((1,), (1,)), ((), ()))


def complex_product(left, right):
    rows, columns, width = left.shape[1], right.shape[1], left.shape[2]
    z = lax.dot_general(
        left.reshape(2 * rows, width),
        right.reshape(2 * columns, width),
        CONTRACT_LAST,
        preferred_element_type=jnp.float32,
    )
    real = z[:rows, :columns] + z[rows:, columns:]
    imag = z[rows:, :columns] - z[:rows, columns:]
    return real.astype(jnp.bfloat16), imag.astype(jnp.bfloat16)


def weighted(block, spectrum):
    return (block.astype(jnp.float32) * spectrum).astype(jnp.bfloat16)


def divided(place_ref, both_ref, keep_ref, send_ref, run):
    side, column, busy = place_ref[0], place_ref[1], place_ref[2] > 0

    def nothing():
        both_ref[...] = jnp.zeros_like(both_ref)

    pl.when(busy & (side == DOWN))(lambda: run(False))
    pl.when(busy & (side == UP))(lambda: run(True))
    pl.when(jnp.logical_not(busy))(nothing)
    keep_ref[...] = both_ref[column]
    send_ref[...] = both_ref[1 - column]


def whole_tiles_body(steps, columns, cores, place_ref, spec_ref, *refs):
    blocks, (keep_ref, send_ref, both_ref) = refs[:-3], refs[-3:]
    mode_count = blocks[0].shape[1]
    per_device = mode_count // (columns * cores)


    def run(up):
        for tile, (x, y) in enumerate(steps):
            left, right = (blocks[y], blocks[x]) if up else (blocks[x], blocks[y])

            @pl.loop(0, mode_count // BAND)
            def _(k):
                band = pl.ds(pl.multiple_of(k * BAND, BAND), BAND)
                part = weighted(right[:, band], spec_ref[tile : tile + 1])
                for kind, product in enumerate(complex_product(left[...], part)):
                    for d in range(columns * cores):
                        share = product[d * per_device : (d + 1) * per_device]
                        both_ref[d // cores, tile, d % cores, kind, :, band] = share

    divided(place_ref, both_ref, keep_ref, send_ref, run)


def chunk_tiles_body(columns, cores, place_ref, spec_ref, *refs):
    blocks, (y_ref, keep_ref, send_ref, both_ref) = refs[:-4], refs[-4:]
    mode_count = blocks[0].shape[1]
    sharers = columns * cores
    per_device = mode_count // sharers
    piece = LANES // sharers

    def run(up):
        for slot in range(len(blocks)):
            for sub in range(y_ref.shape[0]):
                part_y = weighted(y_ref[sub], spec_ref[slot : slot + 1])
                if up:
                    product = complex_product(part_y, blocks[slot][...])
                else:
                    product = complex_product(blocks[slot][...], part_y)
                for part in range(2):
                    for d in range(sharers):
                        at = (d // cores, d % cores, slot, sub, part)
                        if not up:
                            rows = slice(d * per_device, (d + 1) * per_device)
                            both_ref[at] = product[part][rows]
                            continue
                        share = product[part][d * piece : (d + 1) * piece]
                        for b in range(mode_count // LANES):
                            rows = slice(b * piece, (b + 1) * piece)
                            both_ref[at + (rows,)] = share[:, b * LANES : (b + 1) * LANES]

    divided(place_ref, both_ref, keep_ref, send_ref, run)


def kernel_call(body, held, columns, place, specs, arrays, flops):
    vmem = pl.BlockSpec(memory_space=pltpu.VMEM)
    return pl.pallas_call(
        body,
        out_shape=[jax.ShapeDtypeStruct(held, jnp.bfloat16)] * 2,
        in_specs=[pl.BlockSpec(memory_space=pltpu.SMEM)] + [vmem] * (len(arrays) + 1),
        out_specs=[vmem, vmem],
        scratch_shapes=[pltpu.VMEM((columns,) + held, jnp.bfloat16)],
        compiler_params=pltpu.CompilerParams(vmem_limit_bytes=24 * 2**20),
        cost_estimate=pl.CostEstimate(flops=flops, bytes_accessed=0, transcendentals=0),
    )(place, specs, *arrays)


def assemble_body(freqs, cores, place_ref, taper_ref, noise_ref, *refs):
    *refs, out_ref = refs
    whole_kept, whole_come, *chunk_refs = refs
    chunk_pairs = list(zip(chunk_refs[::2], chunk_refs[1::2]))
    subs = [(kept, come, i) for kept, come in chunk_pairs for i in range(kept.shape[1])]
    side, freq = place_ref[0], place_ref[3]
    here_down = []
    per_device, mode_count = whole_kept.shape[2:]
    piece = per_device // len(subs)

    def of(kept, come, from_down, at):
        return (kept if from_down == here_down[-1] else come)[at].astype(jnp.float32)

    def put(sep, part, rows, cols, value):
        taper = taper_ref[sep, rows, cols].astype(jnp.float32)
        noise = noise_ref[sep, rows, part, cols].astype(jnp.float32)
        out_ref[sep, rows, part, cols] = noise if value is None else taper * value + noise

    def column_chunk(slot, j, k, part):
        kept, come, sub = subs[k]
        rows = slice(j * piece, (j + 1) * piece)
        return of(kept, come, True, (slot, sub, part, rows))

    def row_chunk(slot, j, k, part):
        kept, come, sub = subs[j]
        rows = slice(k * piece, (k + 1) * piece)
        return of(kept, come, False, (slot, sub, part, rows))

    def fill(sep, value_of):
        for part in range(2):
            for j in range(len(subs)):
                for k in range(mode_count // LANES):
                    rows = slice(j * piece, (j + 1) * piece)
                    cols = slice(k * LANES, (k + 1) * LANES)
                    put(sep, part, rows, cols, value_of(part, j, k, rows, cols))

    def both_whole(part, j, k, rows, cols):
        at = (0, part, rows, cols)
        return whole_kept[at].astype(jnp.float32) + whole_come[at].astype(jnp.float32)

    def nothing(part, j, k, rows, cols):
        return None

    def low_second(part, j, k, rows, cols):
        return of(whole_kept, whole_come, True, (1, part, rows, cols)) + row_chunk(1, j, k, part)

    def middle_second(part, j, k, rows, cols):
        return of(whole_kept, whole_come, False, (1, part, rows, cols)) + column_chunk(
            1, j, k, part
        )

    def low_third(part, j, k, rows, cols):
        return column_chunk(0, j, k, part) + row_chunk(0, j, k, part)

    pl.when(freq < freqs - 1)(lambda: fill(0, both_whole))
    pl.when(freq == freqs - 1)(lambda: fill(0, nothing))
    for here in (DOWN, UP):
        here_down.append(here == DOWN)
        pl.when((freq == 0) & (side == here))(lambda: fill(1, low_second))
        pl.when((freq == LOW) & (side == here))(lambda: fill(1, middle_second))
        pl.when((freq == 0) & (side == here))(lambda: fill(2, low_third))
    pl.when(freq > LOW)(lambda: fill(1, nothing))
    pl.when(freq > 0)(lambda: fill(2, nothing))


def meet_in_the_middle(beam_matrix, sky_spectrum, taper_tiles, noise_tiles):
    columns, cores = lax.axis_size("ell"), lax.axis_size("pol")
    freqs = lax.axis_size("freq")
    freq, column, side = (lax.axis_index(name) for name in ("freq", "ell", "pol"))
    own = beam_matrix[0]
    mode_count, width = own.shape[1], own.shape[2]
    sharers = columns * cores
    per_device = mode_count // sharers
    chunks = mode_count // LANES
    piece = LANES // sharers
    down = side == DOWN
    first, last = 0, freqs - 1
    meets = ((freq == LOW) & down) | ((freq == HIGH) & ~down)
    outside = ((freq == first) & ~down) | ((freq == last) & down)

    def place_of(busy):
        return jnp.stack([side, column, busy, freq]).astype(jnp.int32)

    def along(block, route):
        pairs = [(f * cores + p, g * cores + q) for (f, p), (g, q) in route]
        return lax.ppermute(block, ("freq", "pol"), pairs)

    def over_columns(block, members):
        pairs = [
            ((f * columns + e) * cores + p, (f * columns + 1 - e) * cores + p)
            for f, p in members
            for e in range(columns)
        ]
        return lax.ppermute(block, ("freq", "ell", "pol"), pairs)

    def other_core(block):
        return lax.ppermute(block, "pol", [(0, 1), (1, 0)])

    def chunk_of(k):
        straight = own[:, k * LANES : (k + 1) * LANES]
        spread = own.reshape(2, sharers, per_device, width)[:, :, k * piece : (k + 1) * piece]
        return jnp.where(down, straight, spread.reshape(2, LANES, width))

    middle = [(LOW, DOWN), (HIGH, UP)]

    below = lax.ppermute(sky_spectrum[0], "freq", [(f, f + 1) for f in range(freqs - 1)])
    below2 = lax.ppermute(sky_spectrum[0], "freq", [(f, f + 2) for f in range(freqs - 2)])

    outer = along(
        own,
        [
            ((first, DOWN), (LOW, DOWN)),
            ((last, UP), (HIGH, UP)),
            ((LOW, UP), (first, UP)),
            ((HIGH, DOWN), (last, DOWN)),
        ],
    )
    near = along(own, [((HIGH, DOWN), (LOW, DOWN)), ((LOW, UP), (HIGH, UP))])
    cuts = [range(0, chunks // 2)] + [range(k, k + 1) for k in range(chunks // 2, chunks)]
    far_chunks = [jnp.stack([chunk_of(k) for k in cut]) for cut in cuts]
    far_chunks, outer, below, below2 = lax.optimization_barrier(
        (far_chunks, outer, below, below2)
    )
    far = [
        along(c, [((last, DOWN), (LOW, DOWN)), ((first, UP), (HIGH, UP))]) for c in far_chunks
    ]

    own_sky = sky_spectrum[0]
    end_specs = jnp.where(down, below[:1], own_sky[:1])
    near_specs = jnp.where(
        down, jnp.stack([below[1], own_sky[0]]), jnp.stack([below[1], below[0]])
    )
    far_specs = jnp.where(
        down, jnp.stack([below[2], own_sky[1]]), jnp.stack([below2[2], below2[1]])
    )

    def after(value, *earlier):
        return lax.optimization_barrier((value, *earlier))[0]

    def whole_tiles(steps, specs, busy, blocks):
        return kernel_call(
            lambda *refs: whole_tiles_body(steps, columns, cores, *refs),
            (len(steps), cores, 2, per_device, mode_count),
            columns,
            place_of(busy),
            specs,
            blocks,
            flops=COST[len(steps)],
        )

    def far_tiles(y):
        return kernel_call(
            lambda *refs: chunk_tiles_body(columns, cores, *refs),
            (cores, 2, y.shape[0], 2, per_device, LANES),
            columns,
            place_of(meets),
            far_specs,
            [outer, own, y],
            flops=COST[2],
        )

    def swapped(pair, members):
        return pair[0], over_columns(pair[1], members)

    def total(pair):
        return (pair[0].astype(jnp.float32) + pair[1].astype(jnp.float32)).astype(jnp.bfloat16)

    def exchanged(by_core):
        kept = lax.dynamic_index_in_dim(by_core, side, 0, keepdims=False)
        return kept, other_core(lax.dynamic_index_in_dim(by_core, 1 - side, 0, keepdims=False))

    def far_home(sums):
        come = along(sums, [((LOW, DOWN), (first, DOWN)), ((HIGH, UP), (first, UP))])
        return jnp.where(at_low & down, sums, come)

    at_low = freq == LOW
    pair = whole_tiles([(0, 1)], end_specs, meets | outside, [outer, own])
    end = swapped(pair, middle + [(first, UP), (last, DOWN)])
    near = after(near, pair[0])
    pair = whole_tiles([(0, 2), (1, 2)], near_specs, meets, [outer, own, near])
    nears = swapped(pair, middle)
    end = total(after(end, pair[0]))[0]

    far0 = far_tiles(after(far[0], end))
    swap0 = swapped(far0, middle)
    near_outer, near_own = total(after(nears, far0[0]))
    come = along(
        jnp.where(down, end, near_own),
        [((LOW, DOWN), (first, DOWN)), ((HIGH, UP), (LOW, UP)), ((last, DOWN), (HIGH, DOWN))],
    )
    second = along(near_outer, [((LOW, DOWN), (first, DOWN)), ((HIGH, UP), (LOW, UP))])
    far1 = far_tiles(after(far[1], near_outer))
    swap1 = swapped(far1, middle)
    sum0 = total(after(swap0, far1[0]))
    home0 = far_home(sum0)
    far2 = far_tiles(after(far[2], sum0))
    swap2 = swapped(far2, middle)
    sum1 = total(after(swap1, far2[0]))
    home1 = far_home(sum1)
    home2 = far_home(total(after(swap2, sum1)))

    first_sep = jnp.where(
        down, jnp.where(at_low, near_own, come), jnp.where(at_low, come, end)
    )
    results = [*exchanged(jnp.stack([first_sep, second], axis=1))]
    for home in (home0, home1, home2):
        results += exchanged(after(home, results[-2]))

    vmem = pl.BlockSpec(memory_space=pltpu.VMEM)
    covariance = pl.pallas_call(
        lambda *refs: assemble_body(freqs, cores, *refs),
        out_shape=jax.ShapeDtypeStruct(noise_tiles.shape[1:], jnp.float32),
        in_specs=[pl.BlockSpec(memory_space=pltpu.SMEM)] + [vmem] * (len(results) + 2),
        out_specs=vmem,
        compiler_params=pltpu.CompilerParams(vmem_limit_bytes=24 * 2**20),
    )(place_of(meets), taper_tiles, noise_tiles[0], *results)
    return covariance[None]


def local(beam_matrix, sky_spectrum, taper_tiles, noise_tiles):
    freqs, columns, cores = (lax.axis_size(name) for name in ("freq", "ell", "pol"))
    separations = sky_spectrum.shape[1]
    mode_count = beam_matrix.shape[2]
    two_below_two_above = freqs == 2 * HIGH and separations == freqs - 1
    halves = columns == 2 and cores == 2
    whole_pieces = mode_count % (LANES * columns * cores) == 0 and mode_count % BAND == 0
    if two_below_two_above and halves and whole_pieces:
        return meet_in_the_middle(beam_matrix, sky_spectrum, taper_tiles, noise_tiles)
    return partners_passed_down(beam_matrix, sky_spectrum, taper_tiles, noise_tiles)


def solution(mesh):
    placed = (
        P(("grp", "freq"), None, None, ("ell", "pol")),
        P(("grp", "freq"), None, ("ell", "pol")),
        P(None, ("ell", "pol"), None),
        P(("grp", "freq"), None, ("ell", "pol"), None, None),
    )
    return jax.shard_map(
        local,
        mesh=mesh,
        in_specs=placed,
        out_specs=P(("grp", "freq"), None, ("ell", "pol"), None, None),
        check_vma=False,
    )
```
